512 devices in a mesh: query: 4 (over x), ctx: 32 (over z_lo, y), ffn: 4 (over z_hi, core).
Axes of the slice: x: 4, y: 4, z: 16 (z_hi: 2, z_lo: 8; z = z_hi * 8 + z_lo), core: 2. Of those that a mesh axis runs over, the one named last changes fastest.
Arguments:
- token_grads: bfloat16 [12288, 14336], P('ctx', 'ffn'), may hold values from -6 to 6
- token_inputs: bfloat16 [12288, 4096], P('ctx', 'ffn'), may hold values from -6 to 6
- up_factors: bfloat16 [4096, 14336], P(('query', 'ctx'), 'ffn'), may hold values from -0.0078125 to 0.0078125
- in_factors: bfloat16 [4096, 4096], P(('query', 'ctx'), 'ffn'), may hold values from -0.09375 to 0.09375
- loss_mask: int32 [12288], P('ctx'), may hold values 0 or 1
Outputs:
- scores: float32 [12288, 128], P(('ctx', 'ffn'), 'query')
The draws below stay inside these ranges and needn't reach their ends.
All inputs are finite; a program needn't handle non-finite values. No bound on the sum of `loss_mask` on one device may be relied on, other than what follows from the above.
Results may differ from the reference program's by a relative error of at most 0.0003.
Values may be sent and summed in bfloat16 or wider, within the bound.
No kernel may reach another device: no remote copies, remote signals or barrier semaphores. Data moves between devices by JAX's collectives and lax.ppermute only.
A program may use at most 64 MiB of HBM per device.

```python
import jax
import jax.numpy as jnp
from jax import lax

D = 4096
FF = 14336
RANK = 32
TOK_DEV = 384
QUERIES = 128
TOKENS = 12288


def with_ends(values, key, smallest, largest):
    place = [jax.random.randint(jax.random.fold_in(key, axis), (), 0, length) for axis, length in enumerate(values.shape)]
    main_axis = values.shape.index(max(values.shape))
    next_to = place[:main_axis] + [(place[main_axis] + 1) % values.shape[main_axis]] + place[main_axis + 1:]
    return values.at[tuple(place)].set(smallest).at[tuple(next_to)].set(largest)


def shard_levels(key, shape, shards, low, largest):
    gain = 1.0
    for axis_at, parts in shards:
        draws = jax.random.uniform(jax.random.fold_in(jax.random.fold_in(key, 6), axis_at), (parts,), jnp.float32, low / len(shards), largest / len(shards))
        gain = gain * jnp.repeat(jnp.exp(draws), shape[axis_at] // parts).reshape((-1,) + (1,) * (len(shape) - 1 - axis_at))
    return gain


def bell_draw(stream_key, dims, width, limit, split=(), dtype=jnp.bfloat16):
    factor_of = shard_levels(stream_key, dims, split, -0.22, 0.18) if split else 1.0
    values = jax.random.normal(stream_key, dims, jnp.float32) * width * factor_of
    return jnp.minimum(jnp.maximum(values, -limit), limit).astype(dtype)


def setup_inputs(seed: int = 0) -> dict:
    keys = jax.random.split(jax.random.key(seed), 6)
    return {
        "token_grads": bell_draw(keys[0], (TOKENS, FF), 1.0, 6.0, ((0, 32), (1, 4))),
        "token_inputs": bell_draw(keys[1], (TOKENS, D), 1.0, 6.0, ((0, 32), (1, 4))),
        "up_factors": bell_draw(keys[2], (QUERIES * RANK, FF), (FF * RANK) ** -0.5, 0.0078125, ((0, 128), (1, 4))),
        "in_factors": bell_draw(keys[3], (QUERIES * RANK, D), D ** -0.5, 0.09375, ((0, 128), (1, 4))),
        "loss_mask": with_ends((jax.random.randint(keys[4], (TOKENS,), 0, 4) < 3).astype(jnp.int32), jax.random.fold_in(keys[4], 1), 0, 1),
    }


def reference(token_grads, token_inputs, up_factors, in_factors, loss_mask):
    block_count = TOKENS // TOK_DEV
    grad_blocks = token_grads.reshape(block_count, TOK_DEV, FF)
    input_blocks = token_inputs.reshape(block_count, TOK_DEV, D)
    mask_blocks = loss_mask.reshape(block_count, TOK_DEV)

    def block_scores(packed):
        grad_rows, input_rows, mask_rows = packed
        left_proj = jnp.dot(grad_rows, up_factors.T, preferred_element_type=jnp.float32)
        right_proj = jnp.dot(input_rows, in_factors.T, preferred_element_type=jnp.float32)
        summed = (left_proj * right_proj).reshape(TOK_DEV, QUERIES, RANK).sum(axis=2)
        return summed * mask_rows.astype(jnp.float32)[:, None]

    result = lax.map(block_scores, (grad_blocks, input_blocks, mask_blocks))
    return result.reshape(TOKENS, QUERIES)
```

```python
import jax
import jax.numpy as jnp
from jax import lax
from jax.sharding import Mesh, PartitionSpec as P

RANK = 32
HALF = RANK // 2
SWAP = ((0, 1), (1, 0))
Z_STEPS = (2, 1)
Z_OFFSETS = (0, 2, 1, 3)
Y_OFFSETS = (0, -1, 1, 2)


def rows_of(data_rows, factor_rows):
    return lax.dot_general(factor_rows, data_rows, (((1,), (1,)), ((), ())), preferred_element_type=jnp.float32)


def shift(value, axis, by):
    return lax.ppermute(value, axis, [((i + by) % 4, i) for i in range(4)])


def flip(value, axis, bits):
    return lax.ppermute(value, axis, [(i, i ^ bits) for i in range(lax.axis_size(axis))])


def swap(value, axis):
    return lax.ppermute(value, axis, SWAP)


def gather_z(block):
    for bits in Z_STEPS:
        block = jnp.concatenate([block, flip(block, "z_quad", bits)], axis=0)
    return block


def gather_y(block):
    return [block] + [shift(block, "y", by) for by in Y_OFFSETS[1:]]


def pair_rows(rows, x_at):
    quarter = rows.shape[0] // 4
    part = swap(lax.dynamic_slice_in_dim(rows, x_at * quarter, quarter, 0), "z_pair")
    return jnp.concatenate([rows, part] + [shift(part, "query", by) for by in (1, 2, 3)], axis=0)


def sum_over_halves(partial):
    count, tokens = partial.shape[0] // HALF, partial.shape[1]
    blocks = partial.reshape(count, HALF, tokens)
    largest = jnp.max(jnp.abs(blocks), axis=1)
    exponent = jnp.clip(jnp.ceil(jnp.log2(jnp.maximum(largest, 1e-30)) + 0.01), -100.0, 100.0)
    coded = jnp.round(blocks * (jnp.exp2(-exponent) * 32766.0)[:, None, :]).astype(jnp.int16)
    sent = jnp.concatenate([coded.reshape(count * HALF, tokens), exponent.astype(jnp.int16)], axis=0)
    got = swap(sent, "z_half").astype(jnp.float32)
    scale = jnp.exp2(got[count * HALF :]) * (1.0 / 32766.0)
    other = got[: count * HALF].reshape(count, HALF, tokens) * scale[:, None, :]
    return blocks + other


def body(token_grads, token_inputs, up_factors, in_factors, loss_mask):
    x_at, y_at, core = lax.axis_index("query"), lax.axis_index("y"), lax.axis_index("core")
    z_half, z_pair = lax.axis_index("z_half"), lax.axis_index("z_pair")
    hidden, features = token_grads.shape[1], token_inputs.shape[1]
    tokens = token_grads.shape[0]
    quarter = tokens // 4

    both = jnp.concatenate([in_factors, up_factors], axis=1)
    kept = lax.dynamic_slice_in_dim(both, core * HALF, HALF, 0)
    got = swap(lax.dynamic_slice_in_dim(both, (1 - core) * HALF, HALF, 0), "core")
    in_block = jnp.concatenate([kept[:, :features], got[:, :features]], axis=1)
    up_block = jnp.concatenate([kept[:, features:], got[:, features:]], axis=1)

    in_all = jnp.concatenate(gather_y(gather_z(in_block)), axis=0)
    inputs = pair_rows(token_inputs, x_at)
    inputs_other = swap(inputs, "core")
    right = rows_of(inputs, in_all[:, :features]) + rows_of(inputs_other, in_all[:, features:])
    right = sum_over_halves(right)

    up_all = jnp.concatenate(gather_y(gather_z(up_block)), axis=0)
    grads = pair_rows(token_grads, x_at)
    grads_other = swap(grads, "core")
    left = rows_of(grads, up_all[:, :hidden]) + rows_of(grads_other, up_all[:, hidden:])

    count = right.shape[0]
    summed = (left.reshape(right.shape) * right).sum(axis=1)
    parts = summed.reshape(count, 2, 4, quarter).transpose(2, 1, 0, 3)
    own, other = parts[:, 0], parts[:, 1]
    other = lax.dynamic_slice_in_dim(jnp.concatenate([other, other], axis=0), (4 - x_at) % 4, 4, 0)
    parts = jnp.stack([own, other], axis=1).reshape(2, 2, 2, count, quarter)

    mine = lax.dynamic_index_in_dim(parts, core, 1, keepdims=False)
    theirs = lax.dynamic_index_in_dim(parts, 1 - core, 1, keepdims=False)
    mine = mine + swap(theirs, "core")
    mine = jnp.stack([mine[:, 0], swap(mine[:, 1], "z_pair")], axis=1)
    result = lax.dynamic_index_in_dim(mine, z_half, 0, keepdims=False)
    result = result + swap(lax.dynamic_index_in_dim(mine, 1 - z_half, 0, keepdims=False), "z_half")
    result = result.reshape(2 * count, quarter)

    at = lax.broadcasted_iota(jnp.int32, (2 * count, 2 * count), 0)
    column = lax.broadcasted_iota(jnp.int32, (2 * count, 2 * count), 1)
    quads = len(Z_OFFSETS)
    z_quad = lax.axis_index("z_quad")
    place = jnp.zeros_like(at)
    for j, y_by in enumerate(Y_OFFSETS):
        for k, bits in enumerate(Z_OFFSETS):
            for pair in range(2):
                row = pair * count + j * quads + k
                to = ((z_quad ^ bits) * 2 + (z_pair ^ pair)) * 4 + (y_at + y_by) % 4
                place = place + jnp.where(at == row, to, 0)
    select = (place == column).astype(jnp.float32)
    scores = lax.dot_general(
        result, select, (((0,), (0,)), ((), ())), precision=lax.Precision.HIGHEST, preferred_element_type=jnp.float32
    )
    share = lax.dynamic_slice_in_dim(loss_mask, (z_half * 2 + core) * quarter, quarter, 0)
    return scores * share.astype(jnp.float32)[:, None]


def solution(mesh):
    devices = mesh.devices.reshape(4, 4, 2, 4, 2, 2)
    split = Mesh(devices, ("query", "z_quad", "z_pair", "y", "z_half", "core"))
    ctx, ffn = ("z_quad", "z_pair", "y"), ("z_half", "core")
    in_specs = (
        P(ctx, ffn),
        P(ctx, ffn),
        P(("query",) + ctx, ffn),
        P(("query",) + ctx, ffn),
        P(ctx),
    )
    return jax.shard_map(body, mesh=split, in_specs=in_specs, out_specs=P(ctx + ffn, "query"), check_vma=False)
```

```python
import jax
import jax.numpy as jnp
from jax import lax
from jax.sharding import Mesh, PartitionSpec as P

RANK = 32
GROUP = 16
SWAP = ((0, 1), (1, 0))
Z_OFFSETS = (0, 4, 2, 6, 1, 5, 3, 7)
TOKENS_BY, FACTORS_BY = 1, 3
Y = ("y_hi", "y_lo")


def rows_of(data_rows, factor_rows):
    return lax.dot_general(factor_rows, data_rows, (((1,), (1,)), ((), ())), preferred_element_type=jnp.float32)


def flip(value, axes, bits):
    return lax.ppermute(value, axes, [(i, i ^ bits) for i in range(lax.axis_size(axes))])


def swap(value, axis):
    return lax.ppermute(value, axis, SWAP)


def grow(block, bits):
    return jnp.concatenate([block, flip(block, "z_lo", bits)], axis=0)


def after(value, done):
    return jnp.where(jnp.isnan(done[0, 0]), jnp.zeros_like(value), value)


def coded_half(partial):
    count, tokens = partial.shape[0] // GROUP, partial.shape[1]
    blocks = partial.reshape(count, GROUP, tokens)
    largest = jnp.max(jnp.abs(blocks), axis=1)
    exponent = jnp.clip(jnp.ceil(jnp.log2(jnp.maximum(largest, 1e-30)) + 0.01), -100.0, 100.0)
    coded = jnp.round(blocks * (jnp.exp2(-exponent) * 32766.0)[:, None, :]).astype(jnp.int16)
    return blocks, jnp.concatenate([coded.reshape(count * GROUP, tokens), exponent.astype(jnp.int16)], axis=0)


def sum_over_halves(blocks, sent):
    count, _, tokens = blocks.shape
    got = swap(sent, "z_half").astype(jnp.float32)
    scale = jnp.exp2(got[count * GROUP :]) * (1.0 / 32766.0)
    return blocks + got[: count * GROUP].reshape(count, GROUP, tokens) * scale[:, None, :]


def scores_of(left, right):
    return (left * right).reshape(-1, RANK, left.shape[1]).sum(axis=1)


def split_sum(near, far, core):
    return jnp.where(core == 0, near, far) + swap(jnp.where(core == 0, far, near), "core")


def body(token_grads, token_inputs, up_factors, in_factors, loss_mask):
    y_at, core, z_half = lax.axis_index(Y), lax.axis_index("core"), lax.axis_index("z_half")
    tokens, quarter = token_grads.shape[0], token_grads.shape[0] // 4

    second = lax.axis_index("y_lo") == 1
    pair_inputs = flip(token_inputs, Y, TOKENS_BY)
    inputs = jnp.where(
        second, jnp.concatenate([pair_inputs, token_inputs], axis=0), jnp.concatenate([token_inputs, pair_inputs], axis=0)
    )
    grads = lax.all_gather(token_grads, "y_lo", axis=0, tiled=True)
    in_near = grow(grow(grow(in_factors, 4), 2), 1)
    in_far = flip(in_near, Y, FACTORS_BY)
    blocks, sent = coded_half(split_sum(rows_of(inputs, in_near), rows_of(inputs, in_far), core))
    right = sum_over_halves(blocks, sent)

    up_near = grow(grow(up_factors, 4), 2)
    next_near = flip(up_near, "z_lo", 1)
    up_far = flip(up_near, Y, FACTORS_BY)
    next_far = flip(next_near, Y, FACTORS_BY)
    right = right.reshape(-1, 2 * tokens)
    other = swap(after(right, up_far[:1, :1] + next_far[:1, :1]), "core")
    right_near, right_far = jnp.where(core == 0, right, other), jnp.where(core == 0, other, right)
    half = right.shape[0] // 2
    left_near, left_far, left_last = lax.optimization_barrier(
        [rows_of(grads, up) for up in (jnp.concatenate([up_near, next_near], axis=0), up_far, next_far)]
    )
    summed = jnp.concatenate(
        [
            scores_of(left_near, right_near),
            scores_of(left_far, right_far[:half]),
            scores_of(left_last, right_far[half:]),
        ],
        axis=0,
    )

    count = summed.shape[0]
    parts = summed.reshape(count, 2, 2, 2, quarter).transpose(2, 3, 1, 0, 4)
    mine = lax.dynamic_index_in_dim(parts, core, 1, keepdims=False)
    mine = mine + swap(lax.dynamic_index_in_dim(parts, 1 - core, 1, keepdims=False), "core")
    own, other = jnp.where(second, mine[:, 1], mine[:, 0]), jnp.where(second, mine[:, 0], mine[:, 1])
    mine = jnp.stack([own, flip(other, Y, TOKENS_BY)], axis=1)
    result = lax.dynamic_index_in_dim(mine, z_half, 0, keepdims=False)
    result = result + swap(lax.dynamic_index_in_dim(mine, 1 - z_half, 0, keepdims=False), "z_half")
    result = result.reshape(2 * count, quarter)

    at = lax.broadcasted_iota(jnp.int32, (2 * count, 2 * count), 0)
    column = lax.broadcasted_iota(jnp.int32, (2 * count, 2 * count), 1)
    z_lo = lax.axis_index("z_lo")
    place = jnp.zeros_like(at)
    for pair in range(2):
        for far in range(2):
            for k, bits in enumerate(Z_OFFSETS):
                row = pair * count + far * len(Z_OFFSETS) + k
                to = (z_lo ^ bits) * 4 + (y_at ^ (pair * TOKENS_BY) ^ (far * FACTORS_BY))
                place = place + jnp.where(at == row, to, 0)
    select = (place == column).astype(jnp.float32)
    scores = lax.dot_general(
        result, select, (((0,), (0,)), ((), ())), precision=lax.Precision.HIGHEST, preferred_element_type=jnp.float32
    )
    share = lax.dynamic_slice_in_dim(loss_mask, (z_half * 2 + core) * quarter, quarter, 0)
    return scores * share.astype(jnp.float32)[:, None]


def solution(mesh):
    split = Mesh(mesh.devices.reshape(4, 8, 2, 2, 2, 2), ("query", "z_lo") + Y + ("z_half", "core"))
    ctx, ffn = ("z_lo",) + Y, ("z_half", "core")
    in_specs = (
        P(ctx, ffn),
        P(ctx, ffn),
        P(("query",) + ctx, ffn),
        P(("query",) + ctx, ffn),
        P(ctx),
    )
    return jax.shard_map(body, mesh=split, in_specs=in_specs, out_specs=P(ctx + ffn, "query"), check_vma=False)
```

```python
import jax
import jax.numpy as jnp
from jax import lax
from jax.sharding import Mesh, PartitionSpec as P

RANK = 32
GROUP = 16
SWAP = ((0, 1), (1, 0))
Z_OFFSETS = (0, 4, 2, 6, 1, 5, 3, 7)
TOKENS_BY, FACTORS_BY = 1, 3
Y = ("y_hi", "y_lo")


def rows_of(data_rows, factor_rows):
    return lax.dot_general(factor_rows, data_rows, (((1,), (1,)), ((), ())), preferred_element_type=jnp.float32)


def flip(value, axes, bits):
    return lax.ppermute(value, axes, [(i, i ^ bits) for i in range(lax.axis_size(axes))])


def swap(value, axis):
    return lax.ppermute(value, axis, SWAP)


def grow(block, bits):
    return jnp.concatenate([block, flip(block, "z_lo", bits)], axis=0)


def after(value, done):
    return jnp.where(jnp.isnan(done[0, 0]), jnp.zeros_like(value), value)


def coded_half(partial):
    count, tokens = partial.shape[0] // GROUP, partial.shape[1]
    blocks = partial.reshape(count, GROUP, tokens)
    largest = jnp.max(jnp.abs(blocks), axis=1)
    exponent = jnp.clip(jnp.ceil(jnp.log2(jnp.maximum(largest, 1e-30)) + 0.01), -100.0, 100.0)
    coded = jnp.round(blocks * (jnp.exp2(-exponent) * 32766.0)[:, None, :]).astype(jnp.int16)
    return blocks, jnp.concatenate([coded.reshape(count * GROUP, tokens), exponent.astype(jnp.int16)], axis=0)


def sum_over_halves(blocks, sent):
    count, _, tokens = blocks.shape
    got = swap(sent, "z_half").astype(jnp.float32)
    scale = jnp.exp2(got[count * GROUP :]) * (1.0 / 32766.0)
    return blocks + got[: count * GROUP].reshape(count, GROUP, tokens) * scale[:, None, :]


def scores_of(left, right):
    return (left * right).reshape(-1, RANK, left.shape[1]).sum(axis=1)


def split_sum(near, far, core):
    return jnp.where(core == 0, near, far) + swap(jnp.where(core == 0, far, near), "core")


def body(token_grads, token_inputs, up_factors, in_factors, loss_mask):
    y_at, core, z_half = lax.axis_index(Y), lax.axis_index("core"), lax.axis_index("z_half")
    tokens, quarter = token_grads.shape[0], token_grads.shape[0] // 4

    second = lax.axis_index("y_lo") == 1
    pair_inputs = flip(token_inputs, Y, TOKENS_BY)
    inputs = jnp.where(
        second, jnp.concatenate([pair_inputs, token_inputs], axis=0), jnp.concatenate([token_inputs, pair_inputs], axis=0)
    )
    grads = lax.all_gather(token_grads, "y_lo", axis=0, tiled=True)
    in_got = flip(in_factors, "z_lo", 4)
    in_near = grow(grow(jnp.concatenate([in_factors, in_got], axis=0), 2), 1)
    in_far = flip(in_near, Y, FACTORS_BY)
    blocks, sent = coded_half(split_sum(rows_of(inputs, in_near), rows_of(inputs, in_far), core))
    right = sum_over_halves(blocks, sent)

    up_near = grow(grow(after(up_factors, in_got), 4), 2)
    next_near = flip(up_near, "z_lo", 1)
    up_far = flip(up_near, Y, FACTORS_BY)
    next_far = flip(next_near, Y, FACTORS_BY)
    left = lax.optimization_barrier(rows_of(grads, jnp.concatenate([up_near, next_near, up_far, next_far], axis=0)))
    right = right.reshape(-1, 2 * tokens)
    half = right.shape[0]
    head, rest = right[: half // 2], right[half // 2 :]
    other = swap(head, "core")
    other = jnp.concatenate([other, swap(after(rest, left[:1, :1] + other[:1, :1]), "core")], axis=0)
    right_near, right_far = jnp.where(core == 0, right, other), jnp.where(core == 0, other, right)
    summed = jnp.concatenate([scores_of(left[:half], right_near), scores_of(left[half:], right_far)], axis=0)

    count = summed.shape[0]
    parts = summed.reshape(count, 2, 2, 2, quarter).transpose(2, 3, 1, 0, 4)
    mine = lax.dynamic_index_in_dim(parts, core, 1, keepdims=False)
    mine = mine + swap(lax.dynamic_index_in_dim(parts, 1 - core, 1, keepdims=False), "core")
    own, other = jnp.where(second, mine[:, 1], mine[:, 0]), jnp.where(second, mine[:, 0], mine[:, 1])
    mine = jnp.stack([own, flip(other, Y, TOKENS_BY)], axis=1)
    result = lax.dynamic_index_in_dim(mine, z_half, 0, keepdims=False)
    result = result + swap(lax.dynamic_index_in_dim(mine, 1 - z_half, 0, keepdims=False), "z_half")
    result = result.reshape(2 * count, quarter)

    at = lax.broadcasted_iota(jnp.int32, (2 * count, 2 * count), 0)
    column = lax.broadcasted_iota(jnp.int32, (2 * count, 2 * count), 1)
    z_lo = lax.axis_index("z_lo")
    place = jnp.zeros_like(at)
    for pair in range(2):
        for far in range(2):
            for k, bits in enumerate(Z_OFFSETS):
                row = pair * count + far * len(Z_OFFSETS) + k
                to = (z_lo ^ bits) * 4 + (y_at ^ (pair * TOKENS_BY) ^ (far * FACTORS_BY))
                place = place + jnp.where(at == row, to, 0)
    select = (place == column).astype(jnp.float32)
    scores = lax.dot_general(
        result, select, (((0,), (0,)), ((), ())), precision=lax.Precision.HIGHEST, preferred_element_type=jnp.float32
    )
    share = lax.dynamic_slice_in_dim(loss_mask, (z_half * 2 + core) * quarter, quarter, 0)
    return scores * share.astype(jnp.float32)[:, None]


def solution(mesh):
    split = Mesh(mesh.devices.reshape(4, 8, 2, 2, 2, 2), ("query", "z_lo") + Y + ("z_half", "core"))
    ctx, ffn = ("z_lo",) + Y, ("z_half", "core")
    in_specs = (
        P(ctx, ffn),
        P(ctx, ffn),
        P(("query",) + ctx, ffn),
        P(("query",) + ctx, ffn),
        P(ctx),
    )
    return jax.shard_map(body, mesh=split, in_specs=in_specs, out_specs=P(ctx + ffn, "query"), check_vma=False)
```

```python
import jax
import jax.numpy as jnp
from jax import lax
from jax.sharding import Mesh, PartitionSpec as P

RANK = 32
GROUP = 16
SWAP = ((0, 1), (1, 0))
Z_OFFSETS = (0, 4, 2, 6, 1, 5, 3, 7)
TOKENS_BY, FACTORS_BY = 1, 3
Y = ("y_hi", "y_lo")


def rows_of(data_rows, factor_rows):
    return lax.dot_general(factor_rows, data_rows, (((1,), (1,)), ((), ())), preferred_element_type=jnp.float32)


def flip(value, axes, bits):
    return lax.ppermute(value, axes, [(i, i ^ bits) for i in range(lax.axis_size(axes))])


def swap(value, axis):
    return lax.ppermute(value, axis, SWAP)


def grow(block, bits):
    return jnp.concatenate([block, flip(block, "z_lo", bits)], axis=0)


def after(value, done):
    return jnp.where(jnp.isnan(done[0, 0]), jnp.zeros_like(value), value)


def coded_half(partial):
    count, tokens = partial.shape[0] // GROUP, partial.shape[1]
    blocks = partial.reshape(count, GROUP, tokens)
    largest = jnp.max(jnp.abs(blocks), axis=1)
    exponent = jnp.clip(jnp.ceil(jnp.log2(jnp.maximum(largest, 1e-30)) + 0.01), -100.0, 100.0)
    coded = jnp.round(blocks * (jnp.exp2(-exponent) * 32766.0)[:, None, :]).astype(jnp.int16)
    return blocks, jnp.concatenate([coded.reshape(count * GROUP, tokens), exponent.astype(jnp.int16)], axis=0)


def sum_over_halves(blocks, sent):
    count, _, tokens = blocks.shape
    got = swap(sent, "z_half").astype(jnp.float32)
    scale = jnp.exp2(got[count * GROUP :]) * (1.0 / 32766.0)
    return blocks + got[: count * GROUP].reshape(count, GROUP, tokens) * scale[:, None, :]


def scores_of(left, right):
    return (left * right).reshape(-1, RANK, left.shape[1]).sum(axis=1)


def split_sum(near, far, core):
    return jnp.where(core == 0, near, far) + swap(jnp.where(core == 0, far, near), "core")


def body(token_grads, token_inputs, up_factors, in_factors, loss_mask):
    y_at, core, z_half = lax.axis_index(Y), lax.axis_index("core"), lax.axis_index("z_half")
    tokens, quarter = token_grads.shape[0], token_grads.shape[0] // 4

    second = lax.axis_index("y_lo") == 1
    pair_inputs = flip(token_inputs, Y, TOKENS_BY)
    inputs = jnp.where(
        second, jnp.concatenate([pair_inputs, token_inputs], axis=0), jnp.concatenate([token_inputs, pair_inputs], axis=0)
    )
    grads = lax.all_gather(token_grads, "y_lo", axis=0, tiled=True)
    in_near = grow(grow(grow(in_factors, 4), 2), 1)
    in_far = flip(in_near, Y, FACTORS_BY)
    blocks, sent = coded_half(split_sum(rows_of(inputs, in_near), rows_of(inputs, in_far), core))
    right = sum_over_halves(blocks, sent)

    up_near = grow(grow(up_factors, 4), 2)
    next_near = flip(up_near, "z_lo", 1)
    up_far = flip(up_near, Y, FACTORS_BY)
    next_far = flip(next_near, Y, FACTORS_BY)
    ups = (jnp.concatenate([up_near, next_near], axis=0), up_far, next_far)
    left_near, left_far, left_last = lax.optimization_barrier([rows_of(grads, up) for up in ups])
    right = after(right.reshape(-1, 2 * tokens), left_near[:1, :1] + left_far[:1, :1] + left_last[:1, :1])
    other = swap(right, "core")
    right_near, right_far = jnp.where(core == 0, right, other), jnp.where(core == 0, other, right)
    half = right.shape[0] // 2
    summed = jnp.concatenate(
        [
            scores_of(left_near, right_near),
            scores_of(left_far, right_far[:half]),
            scores_of(left_last, right_far[half:]),
        ],
        axis=0,
    )

    count = summed.shape[0]
    parts = summed.reshape(count, 2, 2, 2, quarter).transpose(2, 3, 1, 0, 4)
    mine = lax.dynamic_index_in_dim(parts, core, 1, keepdims=False)
    mine = mine + swap(lax.dynamic_index_in_dim(parts, 1 - core, 1, keepdims=False), "core")
    own, other = jnp.where(second, mine[:, 1], mine[:, 0]), jnp.where(second, mine[:, 0], mine[:, 1])
    mine = jnp.stack([own, flip(other, Y, TOKENS_BY)], axis=1)
    result = lax.dynamic_index_in_dim(mine, z_half, 0, keepdims=False)
    result = result + swap(lax.dynamic_index_in_dim(mine, 1 - z_half, 0, keepdims=False), "z_half")
    result = result.reshape(2 * count, quarter)

    at = lax.broadcasted_iota(jnp.int32, (2 * count, 2 * count), 0)
    column = lax.broadcasted_iota(jnp.int32, (2 * count, 2 * count), 1)
    z_lo = lax.axis_index("z_lo")
    place = jnp.zeros_like(at)
    for pair in range(2):
        for far in range(2):
            for k, bits in enumerate(Z_OFFSETS):
                row = pair * count + far * len(Z_OFFSETS) + k
                to = (z_lo ^ bits) * 4 + (y_at ^ (pair * TOKENS_BY) ^ (far * FACTORS_BY))
                place = place + jnp.where(at == row, to, 0)
    select = (place == column).astype(jnp.float32)
    scores = lax.dot_general(
        result, select, (((0,), (0,)), ((), ())), precision=lax.Precision.HIGHEST, preferred_element_type=jnp.float32
    )
    share = lax.dynamic_slice_in_dim(loss_mask, (z_half * 2 + core) * quarter, quarter, 0)
    return scores * share.astype(jnp.float32)[:, None]


def solution(mesh):
    split = Mesh(mesh.devices.reshape(4, 8, 2, 2, 2, 2), ("query", "z_lo") + Y + ("z_half", "core"))
    ctx, ffn = ("z_lo",) + Y, ("z_half", "core")
    in_specs = (
        P(ctx, ffn),
        P(ctx, ffn),
        P(("query",) + ctx, ffn),
        P(("query",) + ctx, ffn),
        P(ctx),
    )
    return jax.shard_map(body, mesh=split, in_specs=in_specs, out_specs=P(ctx + ffn, "query"), check_vma=False)
```

```python
import jax
import jax.numpy as jnp
from jax import lax
from jax.sharding import Mesh, PartitionSpec as P

RANK = 32
GROUP = 16
SWAP = ((0, 1), (1, 0))
Z_OFFSETS = (0, 4, 2, 6, 1, 5, 3, 7)
TOKENS_BY, FACTORS_BY = 1, 3
Y = ("y_hi", "y_lo")


def rows_of(data_rows, factor_rows):
    return lax.dot_general(factor_rows, data_rows, (((1,), (1,)), ((), ())), preferred_element_type=jnp.float32)


def flip(value, axes, bits):
    return lax.ppermute(value, axes, [(i, i ^ bits) for i in range(lax.axis_size(axes))])


def swap(value, axis):
    return lax.ppermute(value, axis, SWAP)


def grow(block, bits):
    return jnp.concatenate([block, flip(block, "z_lo", bits)], axis=0)


def after(value, done):
    return jnp.where(jnp.isnan(done[0, 0]), jnp.zeros_like(value), value)


def coded_half(partial):
    count, tokens = partial.shape[0] // GROUP, partial.shape[1]
    blocks = partial.reshape(count, GROUP, tokens)
    largest = jnp.max(jnp.abs(blocks), axis=1)
    exponent = jnp.clip(jnp.ceil(jnp.log2(jnp.maximum(largest, 1e-30)) + 0.01), -100.0, 100.0)
    coded = jnp.round(blocks * (jnp.exp2(-exponent) * 32766.0)[:, None, :]).astype(jnp.int16)
    return blocks, jnp.concatenate([coded.reshape(count * GROUP, tokens), exponent.astype(jnp.int16)], axis=0)


def sum_over_halves(blocks, sent):
    count, _, tokens = blocks.shape
    got = swap(sent, "z_half").astype(jnp.float32)
    scale = jnp.exp2(got[count * GROUP :]) * (1.0 / 32766.0)
    return blocks + got[: count * GROUP].reshape(count, GROUP, tokens) * scale[:, None, :]


def scores_of(left, right):
    return (left * right).reshape(-1, RANK, left.shape[1]).sum(axis=1)


def split_sum(near, far, core):
    return jnp.where(core == 0, near, far) + swap(jnp.where(core == 0, far, near), "core")


def body(token_grads, token_inputs, up_factors, in_factors, loss_mask):
    y_at, core, z_half = lax.axis_index(Y), lax.axis_index("core"), lax.axis_index("z_half")
    tokens, quarter = token_grads.shape[0], token_grads.shape[0] // 4

    second = lax.axis_index("y_lo") == 1
    pair_inputs = flip(token_inputs, Y, TOKENS_BY)
    inputs = jnp.where(
        second, jnp.concatenate([pair_inputs, token_inputs], axis=0), jnp.concatenate([token_inputs, pair_inputs], axis=0)
    )
    grads = lax.all_gather(token_grads, "y_lo", axis=0, tiled=True)
    in_near = grow(grow(grow(in_factors, 4), 2), 1)
    in_far = flip(in_near, Y, FACTORS_BY)
    blocks, sent = coded_half(split_sum(rows_of(inputs, in_near), rows_of(inputs, in_far), core))
    right = sum_over_halves(blocks, sent)

    up_near = grow(grow(up_factors, 4), 2)
    next_near = flip(up_near, "z_lo", 1)
    up_far = flip(up_near, Y, FACTORS_BY)
    next_far = flip(next_near, Y, FACTORS_BY)
    right = right.reshape(-1, 2 * tokens)
    other = swap(after(right, up_far[:1, :1] + next_far[:1, :1]), "core")
    right_near, right_far = jnp.where(core == 0, right, other), jnp.where(core == 0, other, right)
    ups = jnp.concatenate([up_near, next_near, up_far, next_far], axis=0)
    left = lax.optimization_barrier(rows_of(grads, ups))
    half = right.shape[0]
    summed = jnp.concatenate([scores_of(left[:half], right_near), scores_of(left[half:], right_far)], axis=0)

    count = summed.shape[0]
    parts = summed.reshape(count, 2, 2, 2, quarter).transpose(2, 3, 1, 0, 4)
    mine = lax.dynamic_index_in_dim(parts, core, 1, keepdims=False)
    mine = mine + swap(lax.dynamic_index_in_dim(parts, 1 - core, 1, keepdims=False), "core")
    own, other = jnp.where(second, mine[:, 1], mine[:, 0]), jnp.where(second, mine[:, 0], mine[:, 1])
    mine = jnp.stack([own, flip(other, Y, TOKENS_BY)], axis=1)
    result = lax.dynamic_index_in_dim(mine, z_half, 0, keepdims=False)
    result = result + swap(lax.dynamic_index_in_dim(mine, 1 - z_half, 0, keepdims=False), "z_half")
    result = result.reshape(2 * count, quarter)

    at = lax.broadcasted_iota(jnp.int32, (2 * count, 2 * count), 0)
    column = lax.broadcasted_iota(jnp.int32, (2 * count, 2 * count), 1)
    z_lo = lax.axis_index("z_lo")
    place = jnp.zeros_like(at)
    for pair in range(2):
        for far in range(2):
            for k, bits in enumerate(Z_OFFSETS):
                row = pair * count + far * len(Z_OFFSETS) + k
                to = (z_lo ^ bits) * 4 + (y_at ^ (pair * TOKENS_BY) ^ (far * FACTORS_BY))
                place = place + jnp.where(at == row, to, 0)
    select = (place == column).astype(jnp.float32)
    scores = lax.dot_general(
        result, select, (((0,), (0,)), ((), ())), precision=lax.Precision.HIGHEST, preferred_element_type=jnp.float32
    )
    share = lax.dynamic_slice_in_dim(loss_mask, (z_half * 2 + core) * quarter, quarter, 0)
    return scores * share.astype(jnp.float32)[:, None]


def solution(mesh):
    split = Mesh(mesh.devices.reshape(4, 8, 2, 2, 2, 2), ("query", "z_lo") + Y + ("z_half", "core"))
    ctx, ffn = ("z_lo",) + Y, ("z_half", "core")
    in_specs = (
        P(ctx, ffn),
        P(ctx, ffn),
        P(("query",) + ctx, ffn),
        P(("query",) + ctx, ffn),
        P(ctx),
    )
    return jax.shard_map(body, mesh=split, in_specs=in_specs, out_specs=P(ctx + ffn, "query"), check_vma=False)
```
